128 devices in a mesh: brow: 8 (over x, core), bcol: 16 (over z, y).
Axes of the slice: x: 4, y: 4, z: 4, core: 2. Of those that a mesh axis runs over, the one named last changes fastest.
Arguments:
- fields: bfloat16 [8, 64, 640, 512], P('brow', 'bcol'), may hold values from -6 to 6
- skeleton_index: int32 [8, 64, 384], P('brow', 'bcol'), may hold values from 0 to 639, as said below
- redundant_index: int32 [8, 64, 256], P('brow', 'bcol'), may hold values from 0 to 639, as said below
- neighbours: int32 [8, 64, 6], P('brow', 'bcol'), may hold values from 0 to 8, as said below
- coupling: bfloat16 [8, 64, 2, 256, 6, 384], P('brow', 'bcol'), may hold values from -0.09375 to 0.09375
- back_coupling: bfloat16 [8, 64, 2, 384, 6, 256], P('brow', 'bcol'), may hold values from -0.109375 to 0.109375
- inverse: bfloat16 [8, 64, 2, 256, 256], P('brow', 'bcol'), may hold values from -0.25 to 0.25
Outputs:
- updated: bfloat16 [8, 64, 640, 512], P('brow', 'bcol')
The draws below stay inside these ranges and needn't reach their ends.
Inputs may be any that keep to these rules, and one draw needn't show every extreme that they name: For each box, skeleton_index and redundant_index together name each of its 640 unknowns exactly once. For each box, skeleton_index and redundant_index together name each of its 640 unknowns exactly once. `neighbours`: each box names 6 different positions of its 3 by 3 window of boxes, never the centre 4.
All inputs are finite; a program needn't handle non-finite values.
Results may differ from the reference program's by a relative error of at most 0.0051.
Values may be sent and summed in bfloat16 or wider, within the bound.
A program may use at most 128 MiB of HBM per device.

```python
import jax
import jax.numpy as jnp
from jax import lax

K = 384
R = 256
NB = 6
NRHS = 256
M = 640
GR = 8
GC = 64


def box_orders(key):
    keys = jax.random.split(key, GR * GC)
    orders = jax.vmap(lambda sub: jax.random.permutation(sub, M))(keys)
    return orders.astype(jnp.int32)


def draw_skeleton_index(key, part):
    orders = box_orders(key)
    return orders[:, :K].reshape(GR, GC, K)


def draw_redundant_index(key, part):
    orders = box_orders(key)
    return orders[:, K:].reshape(GR, GC, R)


def draw_neighbours(key, part):
    key = jax.random.fold_in(key, 7)
    keys = jax.random.split(key, GR * GC)
    picks = jax.vmap(lambda sub: jax.random.permutation(sub, 8)[:NB])(keys).astype(jnp.int32)
    codes = picks + (picks >= 4).astype(jnp.int32)
    return codes.reshape(GR, GC, NB)


def block_levels(key, extent, shards, smallest, high):
    def one(position, blocks):
        draws = jax.random.uniform(jax.random.fold_in(jax.random.fold_in(key, 6), position), (blocks,), jnp.float32, smallest / len(shards), high / len(shards))
        return jnp.repeat(jnp.exp(draws), extent[position] // blocks).reshape((-1,) + (1,) * (len(extent) - position - 1))

    level = one(*shards[0])
    for cut in shards[1:]:
        level = level * one(*cut)
    return level


def centred(key, dims, deviation, most, pieces=(), kind=jnp.bfloat16):
    values = deviation * jax.random.normal(key, dims, jnp.float32)
    if pieces:
        values = values * block_levels(key, dims, pieces, -0.22, 0.18)
    return jnp.clip(values, -most, most).astype(kind)


def setup_inputs(seed: int = 0) -> dict:
    key_list = jax.random.split(jax.random.key(seed), 8)
    fields = centred(key_list[0], (GR, GC, M, 2 * NRHS), 1.0, 6.0, ((0, 8), (1, 16)))
    skeleton_index = draw_skeleton_index(jax.random.fold_in(key_list[7], 71), 0)
    redundant_index = draw_redundant_index(jax.random.fold_in(key_list[7], 71), 0)
    neighbours = draw_neighbours(jax.random.fold_in(key_list[7], 71), 0)
    coupling = centred(key_list[4], (GR, GC, 2, R, NB, K), (2 * NB * K) ** -0.5, 0.09375, ((0, 8), (1, 16)))
    back_coupling = centred(key_list[5], (GR, GC, 2, K, NB, R), (2 * NB * R) ** -0.5, 0.109375, ((0, 8), (1, 16)))
    inverse = centred(key_list[6], (GR, GC, 2, R, R), (2 * R) ** -0.5, 0.25, ((0, 8), (1, 16)))
    return {"fields": fields, "skeleton_index": skeleton_index, "redundant_index": redundant_index, "neighbours": neighbours, "coupling": coupling, "back_coupling": back_coupling, "inverse": inverse}


def to_complex(product, rows, half):
    real_part = product[:rows, :half] - product[rows:, half:]
    imag_part = product[:rows, half:] + product[rows:, :half]
    return jnp.concatenate([real_part, imag_part], axis=1)


def widen(field):
    padded = jnp.pad(field, ((1, 1), (0, 0), (0, 0), (0, 0)))
    return jnp.pad(padded, ((0, 0), (1, 1), (0, 0), (0, 0)), mode="wrap")


def select(padded, box, codes, width):
    row_pos = box // GC
    col_pos = box % GC
    zero = jnp.zeros((), jnp.int32)
    window = lax.dynamic_slice(padded, (row_pos, col_pos, zero, zero), (3, 3, width, 2 * NRHS))
    window = window.reshape(9, width, 2 * NRHS)
    return window[codes].reshape(NB * width, 2 * NRHS)


def reference(fields, skeleton_index, redundant_index, neighbours, coupling, back_coupling, inverse):
    boxes = GR * GC
    skel = jnp.take_along_axis(fields, skeleton_index[..., None], axis=2)
    redund = jnp.take_along_axis(fields, redundant_index[..., None], axis=2).astype(jnp.float32)
    padded = widen(skel)
    codes = neighbours.reshape(boxes, NB)
    box_ids = jnp.arange(boxes, dtype=jnp.int32)
    c_flat = coupling.reshape(boxes, 2 * R, NB * K)
    i_flat = inverse.reshape(boxes, 2 * R, R)
    r_flat = redund.reshape(boxes, R, 2 * NRHS)

    def first(item):
        box, code, block, inv_block, red_vals = item
        gathered = select(padded, box, code, K)
        target = red_vals - to_complex(jnp.dot(block, gathered, preferred_element_type=jnp.float32), R, NRHS)
        target_b = target.astype(jnp.bfloat16)
        solved = to_complex(jnp.dot(inv_block, target_b, preferred_element_type=jnp.float32), R, NRHS)
        return solved.astype(jnp.bfloat16)

    solved = lax.map(first, (box_ids, codes, c_flat, i_flat, r_flat))
    solved_pad = widen(solved.reshape(GR, GC, R, 2 * NRHS))
    b_flat = back_coupling.reshape(boxes, 2 * K, NB * R)
    s_flat = skel.reshape(boxes, K, 2 * NRHS)

    def second(item):
        box, code, block, skel_vals = item
        gathered = select(solved_pad, box, code, R)
        change = to_complex(jnp.dot(block, gathered, preferred_element_type=jnp.float32), K, NRHS)
        return (skel_vals.astype(jnp.float32) - change).astype(jnp.bfloat16)

    renewed = lax.map(second, (box_ids, codes, b_flat, s_flat))
    result = jnp.zeros((boxes, M, 2 * NRHS), jnp.bfloat16)
    place = jax.vmap(lambda target, where, values: target.at[where].set(values))
    result = place(result, redundant_index.reshape(boxes, R), solved)
    result = place(result, skeleton_index.reshape(boxes, K), renewed)
    return result.reshape(GR, GC, M, 2 * NRHS)
```

```python
import functools

import jax
import jax.numpy as jnp
from jax import lax
from jax.experimental import pallas as pl
from jax.experimental.pallas import tpu as pltpu
from jax.sharding import PartitionSpec as P

MESH = pl.DeviceIdType.MESH
LANES = 128
OWN, SIB, FAR = 0, 1, 2


def to_complex(product, rows, half):
    real_part = product[:rows, :half] - product[rows:, half:]
    imag_part = product[:rows, half:] + product[rows:, :half]
    return jnp.concatenate([real_part, imag_part], axis=1)


def kernel(
    sizes,
    fields_hbm, skel_idx, red_idx, near, coupling_hbm, back_hbm, inverse_hbm,
    out_hbm,
    fields, coupling, back, inverse, redundant_0, redundant_1,
    skel_0, skel_1, solved_0, solved_1, result,
    load_sem, field_sem, out_sem,
    x_send, x_recv, y_send, y_recv, s_send, s_recv, c_send, c_recv, f_send, f_recv,
):
    rows_mesh, cols_mesh, boxes, K, R, nearby = sizes
    M = K + R
    wide = boxes + 2
    half = LANES
    skel, solved, redundant = (skel_0, skel_1), (solved_0, solved_1), (redundant_0, redundant_1)

    row, col = lax.axis_index("brow"), lax.axis_index("bcol")
    core = lax.rem(row, 2)
    sibling = row + 1 - 2 * core
    across = row - 1 + 2 * core
    has_far = jnp.logical_and(across >= 0, across < rows_mesh)
    up, down = lax.rem(col + 1, cols_mesh), lax.rem(col + cols_mesh - 1, cols_mesh)
    at_sibling, at_far, at_up, at_down = (sibling, col), (across, col), (row, up), (row, down)

    barrier = pltpu.get_barrier_semaphore()
    for device in (at_sibling, at_up, at_down):
        pl.semaphore_signal(barrier, inc=1, device_id=device, device_id_type=MESH)

    @pl.when(has_far)
    def _():
        pl.semaphore_signal(barrier, inc=1, device_id=at_far, device_id_type=MESH)

    def load_fields(b):
        return pltpu.make_async_copy(fields_hbm.at[b], fields.at[b], field_sem.at[b])

    for b in range(boxes):
        load_fields(b).start()
    load_inverse = pltpu.make_async_copy(inverse_hbm, inverse, load_sem.at[0])
    load_coupling = pltpu.make_async_copy(coupling_hbm, coupling, load_sem.at[1])
    load_back = pltpu.make_async_copy(back_hbm, back, load_sem.at[2])
    load_inverse.start()
    load_coupling.start()
    load_back.start()

    def remote(window, source, target, device, send, recv):
        return pltpu.make_async_remote_copy(
            src_ref=window.at[source], dst_ref=window.at[target], send_sem=send, recv_sem=recv,
            device_id=device, device_id_type=MESH,
        )

    def x_copy(window, s, b):
        return remote(window, OWN * wide + 1 + b, FAR * wide + 1 + b, at_far, x_send.at[s, b], x_recv.at[s, b])

    def y_up(window, s):
        return remote(window, OWN * wide + boxes, OWN * wide, at_up, y_send.at[s, 0], y_recv.at[s, 0])

    def y_down(window, s):
        return remote(window, OWN * wide + 1, OWN * wide + boxes + 1, at_down, y_send.at[s, 1], y_recv.at[s, 1])

    def s_copy(window, s, b):
        return remote(window, OWN * wide + 1 + b, SIB * wide + 1 + b, at_sibling, s_send.at[s, b], s_recv.at[s, b])

    def c_up(window, s):
        return remote(window, FAR * wide + boxes, FAR * wide, at_up, c_send.at[s, 0], c_recv.at[s, 0])

    def c_down(window, s):
        return remote(window, FAR * wide + 1, FAR * wide + boxes + 1, at_down, c_send.at[s, 1], c_recv.at[s, 1])

    def f_low(window, s):
        return remote(window, OWN * wide, SIB * wide, at_sibling, f_send.at[s, 0], f_recv.at[s, 0])

    def f_high(window, s):
        return remote(window, OWN * wide + boxes + 1, SIB * wide + boxes + 1, at_sibling, f_send.at[s, 1], f_recv.at[s, 1])

    def forward_corners(window, s):
        @pl.when(has_far)
        def _():
            x_copy(window, s, 0).wait_recv()
            c_down(window, s).start()
            x_copy(window, s, boxes - 1).wait_recv()
            c_up(window, s).start()

    def forward_sides(window, s):
        y_up(window, s).wait_recv()
        f_low(window, s).start()
        y_down(window, s).wait_recv()
        f_high(window, s).start()

    def wait_rest(window, s):
        for b in range(boxes):
            s_copy(window, s, b).wait_recv()
        f_low(window, s).wait_recv()
        f_high(window, s).wait_recv()

        @pl.when(has_far)
        def _():
            for b in range(1, boxes - 1):
                x_copy(window, s, b).wait_recv()
            c_up(window, s).wait_recv()
            c_down(window, s).wait_recv()

    def wait_sends(window, s):
        for b in range(boxes):
            s_copy(window, s, b).wait_send()
        for copy in (y_up, y_down, f_low, f_high):
            copy(window, s).wait_send()

        @pl.when(has_far)
        def _():
            for b in range(boxes):
                x_copy(window, s, b).wait_send()
            c_up(window, s).wait_send()
            c_down(window, s).wait_send()

    @pl.when(jnp.logical_not(has_far))
    def _():
        for window in (*skel, *solved):
            def clear(i, carry, window=window):
                window[FAR * wide + i] = jnp.zeros(window.shape[1:], window.dtype)
                return carry

            lax.fori_loop(0, wide, clear, 0)

    lane = lax.broadcasted_iota(jnp.int32, (LANES, LANES), 1)

    def choose(b):
        blocks = []
        for ref, count in ((skel_idx, K), (red_idx, R)):
            names = ref[pl.ds(b, 1), :]
            for k in range(count // LANES):
                column = jnp.broadcast_to(names[:, k * LANES : (k + 1) * LANES], (LANES, LANES)).T
                pieces = [
                    jnp.where(column == lane + m * LANES, 1.0, 0.0).astype(jnp.bfloat16)
                    for m in range(M // LANES)
                ]
                blocks.append(jnp.concatenate(pieces, axis=1))
        return jnp.concatenate(blocks, axis=0)

    def gather(i, carry):
        b = lax.rem(3 * i, 4)
        load_fields(b).wait()
        taken = jnp.dot(choose(b), fields[b], preferred_element_type=jnp.float32).astype(jnp.bfloat16)
        for h in range(2):
            part = jnp.concatenate(
                [taken[:, h * half : (h + 1) * half], taken[:, (2 + h) * half : (3 + h) * half]], axis=1
            )
            skel[h][OWN * wide + 1 + b] = part[:K]
            redundant[h][b] = part[K:]
        return carry

    lax.fori_loop(0, boxes, gather, 0)

    pl.semaphore_wait(barrier, jnp.where(has_far, 4, 3))

    order = (0, 3, 2, 1)

    def send_x(window, s, which):
        @pl.when(has_far)
        def _():
            for b in which:
                x_copy(window, s, b).start()

    def send_skel(h, s):
        y_up(skel[h], s).start()
        y_down(skel[h], s).start()
        for b in range(boxes):
            s_copy(skel[h], s, b).start()

    def window_index(b, j):
        code = near[b, j]
        line = jnp.where(code >= 3, 1, 0) + jnp.where(code >= 6, 1, 0)
        place = jnp.where(line == 1, OWN, jnp.where(line == 2 * core, FAR, SIB))
        return place * wide + b + code - 3 * line

    def gathered(window, b):
        return jnp.concatenate([window[window_index(b, j)] for j in range(nearby)], axis=0)

    def solve(h, s):
        def body(i, carry):
            b = lax.rem(3 * i, 4)
            block = jnp.concatenate(
                [jnp.concatenate([coupling[b, part, j] for j in range(nearby)], axis=1) for part in range(2)], axis=0
            )
            product = jnp.dot(block, gathered(skel[h], b), preferred_element_type=jnp.float32)
            target = redundant[h][b].astype(jnp.float32) - to_complex(product, R, half)
            target_b = target.astype(jnp.bfloat16)
            full = jnp.dot(inverse[b].reshape(2 * R, R), target_b, preferred_element_type=jnp.float32)
            solved[h][OWN * wide + 1 + b] = to_complex(full, R, half).astype(jnp.bfloat16)

            @pl.when(has_far)
            def _():
                x_copy(solved[h], s, b).start()

            @pl.when(b == 0)
            def _():
                y_down(solved[h], s).start()

            @pl.when(b == boxes - 1)
            def _():
                y_up(solved[h], s).start()

            s_copy(solved[h], s, b).start()
            return carry

        lax.fori_loop(0, boxes, body, 0)

    def place(b):
        names = jnp.concatenate([skel_idx[pl.ds(b, 1), :], red_idx[pl.ds(b, 1), :]], axis=1)
        rows = lax.broadcasted_iota(jnp.int32, (M, M), 0)
        return jnp.where(rows == names, 1.0, 0.0).astype(jnp.bfloat16)

    def write(h, b, part):
        lanes = pl.ds((2 * part + h) * half, half)
        return pltpu.make_async_copy(result.at[b, :, lanes], out_hbm.at[b, :, lanes], out_sem.at[h, part, b])

    def renew(h, midway):
        def body(i, carry):
            b = lax.rem(3 * i, 4)
            block = jnp.concatenate(
                [jnp.concatenate([back[b, part, j] for j in range(nearby)], axis=1) for part in range(2)], axis=0
            )
            product = jnp.dot(block, gathered(solved[h], b), preferred_element_type=jnp.float32)
            kept = skel[h][OWN * wide + 1 + b].astype(jnp.float32) - to_complex(product, K, half)
            stacked = jnp.concatenate([kept.astype(jnp.bfloat16), solved[h][OWN * wide + 1 + b]], axis=0)
            placed = jnp.dot(place(b), stacked, preferred_element_type=jnp.float32).astype(jnp.bfloat16)
            for part in range(2):
                result[b, :, (2 * part + h) * half : (2 * part + h + 1) * half] = placed[
                    :, part * half : (part + 1) * half
                ]
                write(h, b, part).start()
            if midway is not None:
                @pl.when(i == 1)
                def _():
                    midway()
            return carry

        lax.fori_loop(0, boxes, body, 0)

    send_x(skel_0, 0, order)
    send_skel(0, 0)
    forward_corners(skel_0, 0)
    send_x(skel_1, 1, order)
    send_skel(1, 1)
    forward_sides(skel_0, 0)
    load_inverse.wait()
    load_coupling.wait()
    wait_rest(skel_0, 0)
    solve(0, 2)
    forward_corners(skel_1, 1)
    forward_sides(skel_1, 1)
    wait_rest(skel_1, 1)
    solve(1, 3)
    forward_corners(solved_0, 2)
    forward_sides(solved_0, 2)
    load_back.wait()
    wait_rest(solved_0, 2)

    def midway():
        forward_corners(solved_1, 3)
        forward_sides(solved_1, 3)

    renew(0, midway)
    wait_rest(solved_1, 3)
    renew(1, None)
    for s, window in enumerate((skel_0, skel_1, solved_0, solved_1)):
        wait_sends(window, s)
    for h in range(2):
        for b in range(boxes):
            for part in range(2):
                write(h, b, part).wait()


def on_device(
    rows_mesh, cols_mesh,
    fields, skeleton_index, redundant_index, neighbours, coupling, back_coupling, inverse,
):
    _, boxes, M, columns = fields.shape
    K, R, nearby = skeleton_index.shape[2], redundant_index.shape[2], neighbours.shape[2]
    bf16 = jnp.bfloat16
    wide = boxes + 2
    half = columns // 2
    anywhere = pl.BlockSpec(memory_space=pl.ANY)
    vmem = pl.BlockSpec(memory_space=pltpu.VMEM)
    dma = pltpu.SemaphoreType.DMA
    out = pl.pallas_call(
        functools.partial(kernel, (rows_mesh, cols_mesh, boxes, K, R, nearby)),
        out_shape=jax.ShapeDtypeStruct((boxes, M, columns), bf16),
        in_specs=[
            anywhere, vmem, vmem, pl.BlockSpec(memory_space=pltpu.SMEM), anywhere, anywhere, anywhere
        ],
        out_specs=anywhere,
        scratch_shapes=[
            pltpu.VMEM((boxes, M, columns), bf16),
            pltpu.VMEM((boxes, 2, nearby, R, K), bf16),
            pltpu.VMEM((boxes, 2, nearby, K, R), bf16),
            pltpu.VMEM((boxes, 2, R, R), bf16),
            pltpu.VMEM((boxes, R, half), bf16),
            pltpu.VMEM((boxes, R, half), bf16),
            pltpu.VMEM((3 * wide, K, half), bf16),
            pltpu.VMEM((3 * wide, K, half), bf16),
            pltpu.VMEM((3 * wide, R, half), bf16),
            pltpu.VMEM((3 * wide, R, half), bf16),
            pltpu.VMEM((boxes, M, columns), bf16),
            dma((3,)), dma((boxes,)), dma((2, 2, boxes)),
            dma((4, boxes)), dma((4, boxes)), dma((4, 2)), dma((4, 2)), dma((4, boxes)), dma((4, boxes)),
            dma((4, 2)), dma((4, 2)), dma((4, 2)), dma((4, 2)),
        ],
        compiler_params=pltpu.CompilerParams(
            collective_id=0, has_side_effects=True, vmem_limit_bytes=56 * 2**20
        ),
        cost_estimate=pl.CostEstimate(flops=14 * 10**9, bytes_accessed=25 * 10**6, transcendentals=0),
    )(
        fields.reshape(boxes, M, columns),
        skeleton_index.reshape(boxes, K),
        redundant_index.reshape(boxes, R),
        neighbours.reshape(boxes, nearby),
        coupling.reshape(boxes, 2, R, nearby, K).transpose(0, 1, 3, 2, 4),
        back_coupling.reshape(boxes, 2, K, nearby, R).transpose(0, 1, 3, 2, 4),
        inverse.reshape(boxes, 2, R, R),
    )
    return out.reshape(1, boxes, M, columns)


def solution(mesh):
    in_specs = (
        P("brow", "bcol", None, None),
        P("brow", "bcol", None),
        P("brow", "bcol", None),
        P("brow", "bcol", None),
        P("brow", "bcol", None, None, None, None),
        P("brow", "bcol", None, None, None, None),
        P("brow", "bcol", None, None, None),
    )
    out_specs = P("brow", "bcol", None, None)
    body = functools.partial(on_device, mesh.shape["brow"], mesh.shape["bcol"])
    return jax.shard_map(body, mesh=mesh, in_specs=in_specs, out_specs=out_specs, check_vma=False)
```

```python
import functools

import jax
import jax.numpy as jnp
from jax import lax
from jax.experimental import pallas as pl
from jax.experimental.pallas import tpu as pltpu
from jax.sharding import PartitionSpec as P

MESH = pl.DeviceIdType.MESH
LANES = 128
OWN, SIB, FAR = 0, 1, 2


def to_complex(product, rows, half):
    real_part = product[:rows, :half] - product[rows:, half:]
    imag_part = product[:rows, half:] + product[rows:, :half]
    return jnp.concatenate([real_part, imag_part], axis=1)


def kernel(
    sizes,
    fields_hbm, skel_idx, red_idx, near, coupling_hbm, back_hbm, inverse_hbm,
    out_hbm,
    fields, coupling, back, inverse, skel, solved, placing, partial, slots,
    load_sem, field_sem, out_sem,
    x_send, x_recv, y_send, y_recv, s_send, s_recv, c_send, c_recv, f_send, f_recv,
):
    rows_mesh, cols_mesh, boxes, K, R, nearby = sizes
    M = K + R
    wide = boxes + 2
    window = 3 * wide
    last = boxes - 1
    half = LANES
    result = fields

    row, col = lax.axis_index("brow"), lax.axis_index("bcol")
    core = lax.rem(row, 2)
    sibling = row + 1 - 2 * core
    across = row - 1 + 2 * core
    has_far = jnp.logical_and(across >= 0, across < rows_mesh)
    up, down = lax.rem(col + 1, cols_mesh), lax.rem(col + cols_mesh - 1, cols_mesh)
    at_sibling, at_far, at_up, at_down = (sibling, col), (across, col), (row, up), (row, down)

    barrier = pltpu.get_barrier_semaphore()
    for device in (at_sibling, at_up, at_down):
        pl.semaphore_signal(barrier, inc=1, device_id=device, device_id_type=MESH)

    @pl.when(has_far)
    def _():
        pl.semaphore_signal(barrier, inc=1, device_id=at_far, device_id_type=MESH)

    def load_fields(b):
        return pltpu.make_async_copy(fields_hbm.at[b], fields.at[b], field_sem.at[b])

    for b in range(boxes):
        load_fields(b).start()
    named = pl.ds(0, nearby)
    load_inverse = pltpu.make_async_copy(inverse_hbm, inverse, load_sem.at[0])
    load_coupling = pltpu.make_async_copy(coupling_hbm, coupling.at[:, :, named], load_sem.at[1])
    load_back = pltpu.make_async_copy(back_hbm, back.at[:, :, named], load_sem.at[2])
    load_coupling.start()
    load_inverse.start()
    load_back.start()

    def remote(stage, source, target, device, send, recv):
        values, base = (skel, solved)[stage // 2], (stage % 2) * window
        return pltpu.make_async_remote_copy(
            src_ref=values.at[base + source], dst_ref=values.at[base + target], send_sem=send, recv_sem=recv,
            device_id=device, device_id_type=MESH,
        )

    def x_copy(s, b):
        return remote(s, OWN * wide + 1 + b, FAR * wide + 1 + b, at_far, x_send.at[s, b], x_recv.at[s, b])

    def y_up(s):
        return remote(s, OWN * wide + boxes, OWN * wide, at_up, y_send.at[s, 0], y_recv.at[s, 0])

    def y_down(s):
        return remote(s, OWN * wide + 1, OWN * wide + boxes + 1, at_down, y_send.at[s, 1], y_recv.at[s, 1])

    def s_copy(s, b):
        return remote(s, OWN * wide + 1 + b, SIB * wide + 1 + b, at_sibling, s_send.at[s, b], s_recv.at[s, b])

    def c_up(s):
        return remote(s, FAR * wide + boxes, FAR * wide, at_up, c_send.at[s, 0], c_recv.at[s, 0])

    def c_down(s):
        return remote(s, FAR * wide + 1, FAR * wide + boxes + 1, at_down, c_send.at[s, 1], c_recv.at[s, 1])

    def f_low(s):
        return remote(s, OWN * wide, SIB * wide, at_sibling, f_send.at[s, 0], f_recv.at[s, 0])

    def f_high(s):
        return remote(s, OWN * wide + last + 2, SIB * wide + last + 2, at_sibling, f_send.at[s, 1], f_recv.at[s, 1])

    def with_far(action):
        pl.when(has_far)(action)

    def send_x(s, which):
        @with_far
        def _():
            for b in which:
                x_copy(s, b).start()

    def arrive_x(s, which):
        @with_far
        def _():
            for b in which:
                x_copy(s, b).wait_recv()

    def corner_down(s):
        @with_far
        def _():
            x_copy(s, 0).wait_recv()
            c_down(s).start()

    def corner_up(s):
        @with_far
        def _():
            x_copy(s, last).wait_recv()
            c_up(s).start()

    def arrive_low_corner(s):
        with_far(lambda: c_up(s).wait_recv())

    def arrive_high_corner(s):
        with_far(lambda: c_down(s).wait_recv())

    def forward_sides(s):
        y_up(s).wait_recv()
        f_low(s).start()
        y_down(s).wait_recv()
        f_high(s).start()

    def arrive_sides(s):
        f_low(s).wait_recv()
        f_high(s).wait_recv()

    def send_y(s):
        y_up(s).start()
        y_down(s).start()

    def send_s(s):
        for b in range(boxes):
            s_copy(s, b).start()

    def arrive_s(s):
        for b in range(boxes):
            s_copy(s, b).wait_recv()

    def wait_sends(s):
        for b in range(boxes):
            s_copy(s, b).wait_send()
        for copy in (y_up, y_down, f_low, f_high):
            copy(s).wait_send()

        @with_far
        def _():
            for b in range(boxes):
                x_copy(s, b).wait_send()
            c_up(s).wait_send()
            c_down(s).wait_send()

    codes = (3, 2 * 3 * (1 - core), 2 * 3 * core)

    def find_slots(b, carry):
        for line in (OWN, SIB, FAR):
            for place in range(3):
                slot = nearby
                for j in range(nearby):
                    slot = jnp.where(near[b, j] == codes[line] + place, j, slot)
                slots[b, 3 * line + place] = slot
        for blocks in (coupling, back):
            for part in range(2):
                blocks[b, part, nearby] = jnp.zeros(blocks.shape[3:], blocks.dtype)
        return carry

    lax.fori_loop(0, boxes, find_slots, 0)

    @pl.when(jnp.logical_not(has_far))
    def _():
        def clear(i, carry):
            for h in range(2):
                for values in (skel, solved):
                    values[h * window + FAR * wide + i] = jnp.zeros(values.shape[1:], values.dtype)
            return carry

        lax.fori_loop(0, wide, clear, 0)

    lane = lax.broadcasted_iota(jnp.int32, (LANES, LANES), 1)

    def choose(b):
        blocks = []
        for ref, count in ((skel_idx, K), (red_idx, R)):
            names = ref[pl.ds(b, 1), :]
            for k in range(count // LANES):
                column = jnp.broadcast_to(names[:, k * LANES : (k + 1) * LANES], (LANES, LANES)).T
                pieces = [
                    jnp.where(column == lane + m * LANES, 1.0, 0.0).astype(jnp.bfloat16)
                    for m in range(M // LANES)
                ]
                blocks.append(jnp.concatenate(pieces, axis=1))
        return jnp.concatenate(blocks, axis=0)

    def gather(b, carry):
        load_fields(b).wait()
        taken = jnp.dot(choose(b), fields[b], preferred_element_type=jnp.float32)
        for h in range(2):
            part = jnp.concatenate(
                [taken[:, h * half : (h + 1) * half], taken[:, (2 + h) * half : (3 + h) * half]], axis=1
            )
            skel[h * window + OWN * wide + 1 + b] = part[:K].astype(jnp.bfloat16)
            partial[h * boxes + b, :R] = part[K:]
        return carry

    lax.fori_loop(0, boxes, gather, 0)

    def make_placing(b, carry):
        names = jnp.concatenate([skel_idx[pl.ds(b, 1), :], red_idx[pl.ds(b, 1), :]], axis=1)
        rows = lax.broadcasted_iota(jnp.int32, (M, M), 0)
        placing[b] = jnp.where(rows == names, 1.0, 0.0).astype(jnp.bfloat16)
        return carry

    def matrix(blocks, b, places):
        found = [slots[b, place] for place in places]
        return jnp.concatenate(
            [jnp.concatenate([blocks[b, part, slot] for slot in found], axis=1) for part in range(2)], axis=0
        )

    def line_values(values, h, line, b):
        three = values[pl.ds(h * window + line * wide + b, 3)]
        return three.reshape(3 * three.shape[1], three.shape[2])

    def near_part(blocks, values, h, b):
        own = h * window + OWN * wide + b
        vectors = jnp.concatenate([values[own], values[own + 2], line_values(values, h, SIB, b)], axis=0)
        places = (3 * OWN, 3 * OWN + 2, 3 * SIB, 3 * SIB + 1, 3 * SIB + 2)
        product = jnp.dot(matrix(blocks, b, places), vectors, preferred_element_type=jnp.float32)
        return to_complex(product, product.shape[0] // 2, half)

    def far_part(blocks, values, h, b):
        places = (3 * FAR, 3 * FAR + 1, 3 * FAR + 2)
        product = jnp.dot(
            matrix(blocks, b, places), line_values(values, h, FAR, b), preferred_element_type=jnp.float32
        )
        return to_complex(product, product.shape[0] // 2, half)

    def solve_near(h, b):
        partial[h * boxes + b, :R] -= near_part(coupling, skel, h, b)

    def solve_far(h, b):
        target = partial[h * boxes + b, :R] - far_part(coupling, skel, h, b)
        full = jnp.dot(
            inverse[b].reshape(2 * R, R), target.astype(jnp.bfloat16), preferred_element_type=jnp.float32
        )
        solved[h * window + OWN * wide + 1 + b] = to_complex(full, R, half).astype(jnp.bfloat16)

    def renew_near(h, b):
        kept = skel[h * window + OWN * wide + 1 + b].astype(jnp.float32)
        partial[h * boxes + b] = kept - near_part(back, solved, h, b)

    def write(h, b, part):
        lanes = pl.ds((2 * part + h) * half, half)
        return pltpu.make_async_copy(result.at[b, :, lanes], out_hbm.at[b, :, lanes], out_sem.at[h, part, b])

    def renew_far(h, b):
        renewed = partial[h * boxes + b] - far_part(back, solved, h, b)
        stacked = jnp.concatenate(
            [renewed.astype(jnp.bfloat16), solved[h * window + OWN * wide + 1 + b]], axis=0
        )
        placed = jnp.dot(placing[b], stacked, preferred_element_type=jnp.float32).astype(jnp.bfloat16)
        for part in range(2):
            result[b, :, (2 * part + h) * half : (2 * part + h + 1) * half] = placed[
                :, part * half : (part + 1) * half
            ]
            write(h, b, part).start()

    def inner(work, h):
        def body(i, carry):
            work(h, 1 + i)
            return carry

        lax.fori_loop(0, 2, body, 0)

    def outer(work, h):
        def body(i, carry):
            work(h, last * i)
            return carry

        lax.fori_loop(0, 2, body, 0)

    def in_order(work, h, order, before):
        def body(i, carry):
            b = sum(jnp.where(i == k, order[k], 0) for k in range(1, boxes)) + jnp.where(i == 0, order[0], 0)
            for k, action in before.items():
                pl.when(i == k)(action)
            work(h, b)
            return carry

        lax.fori_loop(0, boxes, body, 0)

    pl.semaphore_wait(barrier, jnp.where(has_far, 4, 3))

    send_x(0, (0, last, 1, 2))
    send_y(0)
    send_s(0)
    send_s(1)
    lax.fori_loop(0, boxes, make_placing, 0)
    load_coupling.wait()
    arrive_s(0)
    inner(solve_near, 0)
    corner_down(0)
    arrive_s(1)
    inner(solve_near, 1)
    corner_up(0)
    send_x(1, (0, last))
    forward_sides(0)
    send_y(1)
    arrive_sides(0)
    outer(solve_near, 0)
    arrive_x(0, (1, 2))
    send_x(1, (1, 2))
    load_inverse.wait()

    def before_first():
        arrive_low_corner(0)

    def before_last():
        corner_down(1)
        arrive_high_corner(0)

    in_order(solve_far, 0, (1, 2, 0, last), {2: before_first, 3: before_last})
    send_s(2)
    corner_up(1)
    send_x(2, (0, last, 1, 2))
    send_y(2)
    forward_sides(1)
    load_back.wait()
    arrive_s(2)
    inner(renew_near, 0)
    arrive_sides(1)
    outer(solve_near, 1)
    arrive_x(1, (1, 2))

    def before_low():
        arrive_low_corner(1)

    def after_low():
        send_x(3, (0,))
        y_down(3).start()
        corner_down(2)

    def before_high():
        arrive_high_corner(1)

    in_order(solve_far, 1, (1, 0, 2, last), {1: before_low, 2: after_low, 3: before_high})
    send_x(3, (last, 1, 2))
    y_up(3).start()
    send_s(3)
    corner_up(2)
    forward_sides(2)
    arrive_s(3)
    inner(renew_near, 1)
    arrive_sides(2)
    outer(renew_near, 0)
    corner_down(3)
    arrive_x(2, (1, 2))

    def before_rims():
        corner_up(3)
        arrive_low_corner(2)
        arrive_high_corner(2)

    in_order(renew_far, 0, (1, 2, 0, last), {2: before_rims})
    forward_sides(3)
    arrive_x(3, (1, 2))
    inner(renew_far, 1)
    arrive_sides(3)
    outer(renew_near, 1)
    arrive_low_corner(3)
    arrive_high_corner(3)
    outer(renew_far, 1)
    for s in range(4):
        wait_sends(s)
    for h in range(2):
        for b in range(boxes):
            for part in range(2):
                write(h, b, part).wait()


def on_device(
    rows_mesh, cols_mesh,
    fields, skeleton_index, redundant_index, neighbours, coupling, back_coupling, inverse,
):
    _, boxes, M, columns = fields.shape
    K, R, nearby = skeleton_index.shape[2], redundant_index.shape[2], neighbours.shape[2]
    bf16 = jnp.bfloat16
    wide = boxes + 2
    half = columns // 2
    anywhere = pl.BlockSpec(memory_space=pl.ANY)
    vmem = pl.BlockSpec(memory_space=pltpu.VMEM)
    dma = pltpu.SemaphoreType.DMA
    out = pl.pallas_call(
        functools.partial(kernel, (rows_mesh, cols_mesh, boxes, K, R, nearby)),
        out_shape=jax.ShapeDtypeStruct((boxes, M, columns), bf16),
        in_specs=[
            anywhere, vmem, vmem, pl.BlockSpec(memory_space=pltpu.SMEM), anywhere, anywhere, anywhere
        ],
        out_specs=anywhere,
        scratch_shapes=[
            pltpu.VMEM((boxes, M, columns), bf16),
            pltpu.VMEM((boxes, 2, nearby + 1, R, K), bf16),
            pltpu.VMEM((boxes, 2, nearby + 1, K, R), bf16),
            pltpu.VMEM((boxes, 2, R, R), bf16),
            pltpu.VMEM((2 * 3 * wide, K, half), bf16),
            pltpu.VMEM((2 * 3 * wide, R, half), bf16),
            pltpu.VMEM((boxes, M, M), bf16),
            pltpu.VMEM((2 * boxes, K, half), jnp.float32),
            pltpu.SMEM((boxes, 9), jnp.int32),
            dma((3,)), dma((boxes,)), dma((2, 2, boxes)),
            dma((4, boxes)), dma((4, boxes)), dma((4, 2)), dma((4, 2)), dma((4, boxes)), dma((4, boxes)),
            dma((4, 2)), dma((4, 2)), dma((4, 2)), dma((4, 2)),
        ],
        compiler_params=pltpu.CompilerParams(
            collective_id=0, has_side_effects=True, vmem_limit_bytes=48 * 2**20
        ),
        cost_estimate=pl.CostEstimate(flops=14 * 10**9, bytes_accessed=25 * 10**6, transcendentals=0),
    )(
        fields.reshape(boxes, M, columns),
        skeleton_index.reshape(boxes, K),
        redundant_index.reshape(boxes, R),
        neighbours.reshape(boxes, nearby),
        coupling.reshape(boxes, 2, R, nearby, K).transpose(0, 1, 3, 2, 4),
        back_coupling.reshape(boxes, 2, K, nearby, R).transpose(0, 1, 3, 2, 4),
        inverse.reshape(boxes, 2, R, R),
    )
    return out.reshape(1, boxes, M, columns)


def solution(mesh):
    in_specs = (
        P("brow", "bcol", None, None),
        P("brow", "bcol", None),
        P("brow", "bcol", None),
        P("brow", "bcol", None),
        P("brow", "bcol", None, None, None, None),
        P("brow", "bcol", None, None, None, None),
        P("brow", "bcol", None, None, None),
    )
    out_specs = P("brow", "bcol", None, None)
    body = functools.partial(on_device, mesh.shape["brow"], mesh.shape["bcol"])
    return jax.shard_map(body, mesh=mesh, in_specs=in_specs, out_specs=out_specs, check_vma=False)
```

```python
import functools

import jax
import jax.numpy as jnp
from jax import lax
from jax.experimental import pallas as pl
from jax.experimental.pallas import tpu as pltpu
from jax.sharding import PartitionSpec as P

MESH = pl.DeviceIdType.MESH
LANES = 128
OWN, SIB, FAR = 0, 1, 2


def to_complex(product, rows, half):
    real_part = product[:rows, :half] - product[rows:, half:]
    imag_part = product[:rows, half:] + product[rows:, :half]
    return jnp.concatenate([real_part, imag_part], axis=1)


def kernel(
    sizes,
    fields_hbm, skel_hbm, red_hbm, near_hbm, coupling_hbm, back_hbm, inverse_hbm,
    result,
    fields, skel_idx, red_idx, near, coupling, back, inverse, skel, solved, placing, partial, slots,
    load_sem, field_sem,
    x_send, x_recv, y_send, y_recv, s_send, s_recv, c_send, c_recv, f_send, f_recv,
):
    rows_mesh, cols_mesh, boxes, K, R, nearby = sizes
    M = K + R
    wide = boxes + 2
    window = 3 * wide
    last = boxes - 1
    half = LANES

    row, col = lax.axis_index("brow"), lax.axis_index("bcol")
    core = lax.rem(row, 2)
    sibling = row + 1 - 2 * core
    across = row - 1 + 2 * core
    has_far = jnp.logical_and(across >= 0, across < rows_mesh)
    up, down = lax.rem(col + 1, cols_mesh), lax.rem(col + cols_mesh - 1, cols_mesh)
    at_sibling, at_far, at_up, at_down = (sibling, col), (across, col), (row, up), (row, down)

    barrier = pltpu.get_barrier_semaphore()
    for device in (at_sibling, at_up, at_down):
        pl.semaphore_signal(barrier, inc=1, device_id=device, device_id_type=MESH)

    @pl.when(has_far)
    def _():
        pl.semaphore_signal(barrier, inc=1, device_id=at_far, device_id_type=MESH)

    def load_fields(b):
        return pltpu.make_async_copy(fields_hbm.at[b], fields.at[b], field_sem.at[b])

    loads = [
        pltpu.make_async_copy(source, target, load_sem.at[3 + k])
        for k, (source, target) in enumerate(((skel_hbm, skel_idx), (red_hbm, red_idx), (near_hbm, near)))
    ]
    for load in loads:
        load.start()
    for b in range(boxes):
        load_fields(b).start()
    named = pl.ds(0, nearby)
    load_inverse = pltpu.make_async_copy(inverse_hbm, inverse, load_sem.at[0])
    load_coupling = pltpu.make_async_copy(coupling_hbm, coupling.at[:, :, named], load_sem.at[1])
    load_back = pltpu.make_async_copy(back_hbm, back.at[:, :, named], load_sem.at[2])
    load_coupling.start()
    load_inverse.start()
    load_back.start()

    def remote(stage, source, target, device, send, recv):
        values, base = (skel, solved)[stage // 2], (stage % 2) * window
        return pltpu.make_async_remote_copy(
            src_ref=values.at[base + source], dst_ref=values.at[base + target], send_sem=send, recv_sem=recv,
            device_id=device, device_id_type=MESH,
        )

    def x_copy(s, b):
        return remote(s, OWN * wide + 1 + b, FAR * wide + 1 + b, at_far, x_send.at[s, b], x_recv.at[s, b])

    def y_up(s):
        return remote(s, OWN * wide + boxes, OWN * wide, at_up, y_send.at[s, 0], y_recv.at[s, 0])

    def y_down(s):
        return remote(s, OWN * wide + 1, OWN * wide + boxes + 1, at_down, y_send.at[s, 1], y_recv.at[s, 1])

    def s_copy(s, b):
        return remote(s, OWN * wide + 1 + b, SIB * wide + 1 + b, at_sibling, s_send.at[s, b], s_recv.at[s, b])

    def c_up(s):
        return remote(s, FAR * wide + boxes, FAR * wide, at_up, c_send.at[s, 0], c_recv.at[s, 0])

    def c_down(s):
        return remote(s, FAR * wide + 1, FAR * wide + boxes + 1, at_down, c_send.at[s, 1], c_recv.at[s, 1])

    def f_low(s):
        return remote(s, OWN * wide, SIB * wide, at_sibling, f_send.at[s, 0], f_recv.at[s, 0])

    def f_high(s):
        return remote(s, OWN * wide + last + 2, SIB * wide + last + 2, at_sibling, f_send.at[s, 1], f_recv.at[s, 1])

    def with_far(action):
        pl.when(has_far)(action)

    def send_x(s, which):
        @with_far
        def _():
            for b in which:
                x_copy(s, b).start()

    def arrive_x(s, which):
        @with_far
        def _():
            for b in which:
                x_copy(s, b).wait_recv()

    def corner_down(s):
        @with_far
        def _():
            x_copy(s, 0).wait_recv()
            c_down(s).start()

    def corner_up(s):
        @with_far
        def _():
            x_copy(s, last).wait_recv()
            c_up(s).start()

    def arrive_low_corner(s):
        with_far(lambda: c_up(s).wait_recv())

    def arrive_high_corner(s):
        with_far(lambda: c_down(s).wait_recv())

    def forward_sides(s):
        y_up(s).wait_recv()
        f_low(s).start()
        y_down(s).wait_recv()
        f_high(s).start()

    def arrive_sides(s):
        f_low(s).wait_recv()
        f_high(s).wait_recv()

    def send_y(s):
        y_up(s).start()
        y_down(s).start()

    def send_s(s):
        for b in range(boxes):
            s_copy(s, b).start()

    def arrive_s(s):
        for b in range(boxes):
            s_copy(s, b).wait_recv()

    def wait_sends(s):
        for b in range(boxes):
            s_copy(s, b).wait_send()
        for copy in (y_up, y_down, f_low, f_high):
            copy(s).wait_send()

        @with_far
        def _():
            for b in range(boxes):
                x_copy(s, b).wait_send()
            c_up(s).wait_send()
            c_down(s).wait_send()

    codes = (3, 2 * 3 * (1 - core), 2 * 3 * core)

    def find_slots(b, carry):
        for line in (OWN, SIB, FAR):
            for place in range(3):
                slot = nearby
                for j in range(nearby):
                    slot = jnp.where(near[b, j] == codes[line] + place, j, slot)
                slots[b, 3 * line + place] = slot
        for blocks in (coupling, back):
            for part in range(2):
                blocks[b, part, nearby] = jnp.zeros(blocks.shape[3:], blocks.dtype)
        return carry

    for load in loads:
        load.wait()
    lax.fori_loop(0, boxes, find_slots, 0)

    @pl.when(jnp.logical_not(has_far))
    def _():
        def clear(i, carry):
            for h in range(2):
                for values in (skel, solved):
                    values[h * window + FAR * wide + i] = jnp.zeros(values.shape[1:], values.dtype)
            return carry

        lax.fori_loop(0, wide, clear, 0)

    lane = lax.broadcasted_iota(jnp.int32, (LANES, LANES), 1)

    def choose(b):
        blocks = []
        for ref, count in ((skel_idx, K), (red_idx, R)):
            names = ref[pl.ds(b, 1), :]
            for k in range(count // LANES):
                column = jnp.broadcast_to(names[:, k * LANES : (k + 1) * LANES], (LANES, LANES)).T
                pieces = [
                    jnp.where(column == lane + m * LANES, 1.0, 0.0).astype(jnp.bfloat16)
                    for m in range(M // LANES)
                ]
                blocks.append(jnp.concatenate(pieces, axis=1))
        return jnp.concatenate(blocks, axis=0)

    def gather(b, carry):
        load_fields(b).wait()
        taken = jnp.dot(choose(b), fields[b], preferred_element_type=jnp.float32)
        for h in range(2):
            part = jnp.concatenate(
                [taken[:, h * half : (h + 1) * half], taken[:, (2 + h) * half : (3 + h) * half]], axis=1
            )
            skel[h * window + OWN * wide + 1 + b] = part[:K].astype(jnp.bfloat16)
            partial[h * boxes + b, :R] = part[K:]
        return carry

    lax.fori_loop(0, boxes, gather, 0)

    def make_placing(b, carry):
        names = jnp.concatenate([skel_idx[pl.ds(b, 1), :], red_idx[pl.ds(b, 1), :]], axis=1)
        rows = lax.broadcasted_iota(jnp.int32, (M, M), 0)
        placing[b] = jnp.where(rows == names, 1.0, 0.0).astype(jnp.bfloat16)
        return carry

    def matrix(blocks, b, places):
        found = [slots[b, place] for place in places]
        return jnp.concatenate(
            [jnp.concatenate([blocks[b, part, slot] for slot in found], axis=1) for part in range(2)], axis=0
        )

    def line_values(values, h, line, b):
        three = values[pl.ds(h * window + line * wide + b, 3)]
        return three.reshape(3 * three.shape[1], three.shape[2])

    def near_part(blocks, values, h, b):
        own = h * window + OWN * wide + b
        vectors = jnp.concatenate([values[own], values[own + 2], line_values(values, h, SIB, b)], axis=0)
        places = (3 * OWN, 3 * OWN + 2, 3 * SIB, 3 * SIB + 1, 3 * SIB + 2)
        product = jnp.dot(matrix(blocks, b, places), vectors, preferred_element_type=jnp.float32)
        return to_complex(product, product.shape[0] // 2, half)

    def far_part(blocks, values, h, b):
        places = (3 * FAR, 3 * FAR + 1, 3 * FAR + 2)
        product = jnp.dot(
            matrix(blocks, b, places), line_values(values, h, FAR, b), preferred_element_type=jnp.float32
        )
        return to_complex(product, product.shape[0] // 2, half)

    def solve_near(h, bs):
        for b in bs:
            partial[h * boxes + b, :R] -= near_part(coupling, skel, h, b)

    def solve_far(h, bs):
        targets = [
            (partial[h * boxes + b, :R] - far_part(coupling, skel, h, b)).astype(jnp.bfloat16) for b in bs
        ]
        for b, target in zip(bs, targets):
            full = jnp.dot(inverse[b].reshape(2 * R, R), target, preferred_element_type=jnp.float32)
            solved[h * window + OWN * wide + 1 + b] = to_complex(full, R, half).astype(jnp.bfloat16)

    def renew_near(h, bs):
        for b in bs:
            kept = skel[h * window + OWN * wide + 1 + b].astype(jnp.float32)
            partial[h * boxes + b] = kept - near_part(back, solved, h, b)

    def renew_far(h, bs):
        renewed = [
            (partial[h * boxes + b] - far_part(back, solved, h, b)).astype(jnp.bfloat16) for b in bs
        ]
        for b, kept in zip(bs, renewed):
            stacked = jnp.concatenate([kept, solved[h * window + OWN * wide + 1 + b]], axis=0)
            placed = jnp.dot(placing[b], stacked, preferred_element_type=jnp.float32).astype(jnp.bfloat16)
            for part in range(2):
                result[b, :, (2 * part + h) * half : (2 * part + h + 1) * half] = placed[
                    :, part * half : (part + 1) * half
                ]

    inner, outer = (1, 2), (0, last)

    pl.semaphore_wait(barrier, jnp.where(has_far, 4, 3))

    send_x(0, (0, last, 1, 2))
    send_y(0)
    send_s(0)
    send_s(1)
    lax.fori_loop(0, boxes, make_placing, 0)
    load_coupling.wait()
    arrive_s(0)
    solve_near(0, inner)
    corner_down(0)
    arrive_s(1)
    solve_near(1, inner)
    corner_up(0)
    send_x(1, outer)
    forward_sides(0)
    send_y(1)
    arrive_sides(0)
    solve_near(0, outer)
    arrive_x(0, inner)
    send_x(1, inner)
    load_inverse.wait()
    solve_far(0, inner)
    corner_down(1)
    arrive_low_corner(0)
    arrive_high_corner(0)
    solve_far(0, outer)
    send_s(2)
    corner_up(1)
    send_x(2, (0, last, 1, 2))
    send_y(2)
    forward_sides(1)
    load_back.wait()
    arrive_s(2)
    renew_near(0, inner)
    arrive_sides(1)
    solve_near(1, outer)
    arrive_x(1, inner)
    solve_far(1, inner)
    send_x(3, (1,))
    corner_down(2)
    arrive_low_corner(1)
    arrive_high_corner(1)
    solve_far(1, outer)
    send_x(3, (0, last, 2))
    send_s(3)
    corner_up(2)
    send_y(3)
    forward_sides(2)
    arrive_s(3)
    renew_near(1, inner)
    arrive_sides(2)
    renew_near(0, outer)
    corner_down(3)
    arrive_x(2, inner)
    renew_far(0, inner)
    corner_up(3)
    arrive_low_corner(2)
    arrive_high_corner(2)
    renew_far(0, outer)
    forward_sides(3)
    arrive_x(3, inner)
    renew_far(1, inner)
    arrive_sides(3)
    renew_near(1, outer)
    arrive_low_corner(3)
    arrive_high_corner(3)
    renew_far(1, outer)
    for s in range(4):
        wait_sends(s)


def on_device(
    rows_mesh, cols_mesh,
    fields, skeleton_index, redundant_index, neighbours, coupling, back_coupling, inverse,
):
    _, boxes, M, columns = fields.shape
    K, R, nearby = skeleton_index.shape[2], redundant_index.shape[2], neighbours.shape[2]
    bf16 = jnp.bfloat16
    wide = boxes + 2
    half = columns // 2
    far_memory = pl.BlockSpec(memory_space=pltpu.HBM)
    dma = pltpu.SemaphoreType.DMA
    out = pl.pallas_call(
        functools.partial(kernel, (rows_mesh, cols_mesh, boxes, K, R, nearby)),
        out_shape=pltpu.VMEM((boxes, M, columns), bf16),
        in_specs=[far_memory] * 7,
        out_specs=pl.BlockSpec(memory_space=pltpu.VMEM),
        scratch_shapes=[
            pltpu.VMEM((boxes, M, columns), bf16),
            pltpu.VMEM((boxes, K), jnp.int32),
            pltpu.VMEM((boxes, R), jnp.int32),
            pltpu.SMEM((boxes, nearby), jnp.int32),
            pltpu.VMEM((boxes, 2, nearby + 1, R, K), bf16),
            pltpu.VMEM((boxes, 2, nearby + 1, K, R), bf16),
            pltpu.VMEM((boxes, 2, R, R), bf16),
            pltpu.VMEM((2 * 3 * wide, K, half), bf16),
            pltpu.VMEM((2 * 3 * wide, R, half), bf16),
            pltpu.VMEM((boxes, M, M), bf16),
            pltpu.VMEM((2 * boxes, K, half), jnp.float32),
            pltpu.SMEM((boxes, 9), jnp.int32),
            dma((6,)), dma((boxes,)),
            dma((4, boxes)), dma((4, boxes)), dma((4, 2)), dma((4, 2)), dma((4, boxes)), dma((4, boxes)),
            dma((4, 2)), dma((4, 2)), dma((4, 2)), dma((4, 2)),
        ],
        compiler_params=pltpu.CompilerParams(
            collective_id=0, has_side_effects=True, vmem_limit_bytes=56 * 2**20
        ),
        cost_estimate=pl.CostEstimate(flops=14 * 10**9, bytes_accessed=25 * 10**6, transcendentals=0),
    )(
        fields.reshape(boxes, M, columns),
        skeleton_index.reshape(boxes, K),
        redundant_index.reshape(boxes, R),
        neighbours.reshape(boxes, nearby),
        coupling.reshape(boxes, 2, R, nearby, K).transpose(0, 1, 3, 2, 4),
        back_coupling.reshape(boxes, 2, K, nearby, R).transpose(0, 1, 3, 2, 4),
        inverse.reshape(boxes, 2, R, R),
    )
    return out.reshape(1, boxes, M, columns)


def solution(mesh):
    in_specs = (
        P("brow", "bcol", None, None),
        P("brow", "bcol", None),
        P("brow", "bcol", None),
        P("brow", "bcol", None),
        P("brow", "bcol", None, None, None, None),
        P("brow", "bcol", None, None, None, None),
        P("brow", "bcol", None, None, None),
    )
    out_specs = P("brow", "bcol", None, None)
    body = functools.partial(on_device, mesh.shape["brow"], mesh.shape["bcol"])
    return jax.shard_map(body, mesh=mesh, in_specs=in_specs, out_specs=out_specs, check_vma=False)
```

```python
import functools

import jax
import jax.numpy as jnp
from jax import lax
from jax.experimental import pallas as pl
from jax.experimental.pallas import tpu as pltpu
from jax.sharding import PartitionSpec as P

MESH = pl.DeviceIdType.MESH
LANES = 128
OWN, SIB, FAR = 0, 1, 2


def to_complex(product, rows, half):
    real_part = product[:rows, :half] - product[rows:, half:]
    imag_part = product[:rows, half:] + product[rows:, :half]
    return jnp.concatenate([real_part, imag_part], axis=1)


def kernel(
    sizes,
    fields_hbm, skel_hbm, red_hbm, near_hbm, coupling_hbm, back_hbm, inverse_hbm,
    result,
    fields, skel_idx, red_idx, near, coupling, back, inverse, skel, solved, placing, partial, slots,
    load_sem, field_sem,
    x_send, x_recv, y_send, y_recv, s_send, s_recv, c_send, c_recv, f_send, f_recv,
):
    rows_mesh, cols_mesh, boxes, K, R, nearby = sizes
    M = K + R
    wide = boxes + 2
    window = 3 * wide
    last = boxes - 1
    half = LANES

    row, col = lax.axis_index("brow"), lax.axis_index("bcol")
    core = lax.rem(row, 2)
    sibling = row + 1 - 2 * core
    across = row - 1 + 2 * core
    has_far = jnp.logical_and(across >= 0, across < rows_mesh)
    up, down = lax.rem(col + 1, cols_mesh), lax.rem(col + cols_mesh - 1, cols_mesh)
    at_sibling, at_far, at_up, at_down = (sibling, col), (across, col), (row, up), (row, down)

    barrier = pltpu.get_barrier_semaphore()
    for device in (at_sibling, at_up, at_down):
        pl.semaphore_signal(barrier, inc=1, device_id=device, device_id_type=MESH)

    @pl.when(has_far)
    def _():
        pl.semaphore_signal(barrier, inc=1, device_id=at_far, device_id_type=MESH)

    def load_fields(b):
        return pltpu.make_async_copy(fields_hbm.at[b], fields.at[b], field_sem.at[b])

    loads = [
        pltpu.make_async_copy(source, target, load_sem.at[3 + k])
        for k, (source, target) in enumerate(((skel_hbm, skel_idx), (red_hbm, red_idx), (near_hbm, near)))
    ]
    for load in loads:
        load.start()
    inner, outer = (1, 2), (0, last)
    for b in (*outer, *inner):
        load_fields(b).start()
    named = pl.ds(0, nearby)
    load_inverse = pltpu.make_async_copy(inverse_hbm, inverse, load_sem.at[0])
    load_coupling = pltpu.make_async_copy(coupling_hbm, coupling.at[:, :, named], load_sem.at[1])
    load_back = pltpu.make_async_copy(back_hbm, back.at[:, :, named], load_sem.at[2])
    load_coupling.start()
    load_inverse.start()
    load_back.start()

    def remote(stage, source, target, device, send, recv):
        values, base = (skel, solved)[stage // 2], (stage % 2) * window
        return pltpu.make_async_remote_copy(
            src_ref=values.at[base + source], dst_ref=values.at[base + target], send_sem=send, recv_sem=recv,
            device_id=device, device_id_type=MESH,
        )

    def x_copy(s, b):
        return remote(s, OWN * wide + 1 + b, FAR * wide + 1 + b, at_far, x_send.at[s, b], x_recv.at[s, b])

    def y_up(s):
        return remote(s, OWN * wide + boxes, OWN * wide, at_up, y_send.at[s, 0], y_recv.at[s, 0])

    def y_down(s):
        return remote(s, OWN * wide + 1, OWN * wide + boxes + 1, at_down, y_send.at[s, 1], y_recv.at[s, 1])

    def s_copy(s, b):
        return remote(s, OWN * wide + 1 + b, SIB * wide + 1 + b, at_sibling, s_send.at[s, b], s_recv.at[s, b])

    def c_up(s):
        return remote(s, FAR * wide + boxes, FAR * wide, at_up, c_send.at[s, 0], c_recv.at[s, 0])

    def c_down(s):
        return remote(s, FAR * wide + 1, FAR * wide + boxes + 1, at_down, c_send.at[s, 1], c_recv.at[s, 1])

    def f_low(s):
        return remote(s, OWN * wide, SIB * wide, at_sibling, f_send.at[s, 0], f_recv.at[s, 0])

    def f_high(s):
        return remote(s, OWN * wide + last + 2, SIB * wide + last + 2, at_sibling, f_send.at[s, 1], f_recv.at[s, 1])

    def with_far(action):
        pl.when(has_far)(action)

    def send_x(s, which):
        @with_far
        def _():
            for b in which:
                x_copy(s, b).start()

    def arrive_x(s, which):
        @with_far
        def _():
            for b in which:
                x_copy(s, b).wait_recv()

    def corner_down(s):
        @with_far
        def _():
            x_copy(s, 0).wait_recv()
            c_down(s).start()

    def corner_up(s):
        @with_far
        def _():
            x_copy(s, last).wait_recv()
            c_up(s).start()

    def arrive_low_corner(s):
        with_far(lambda: c_up(s).wait_recv())

    def arrive_high_corner(s):
        with_far(lambda: c_down(s).wait_recv())

    def forward_sides(s):
        y_up(s).wait_recv()
        f_low(s).start()
        y_down(s).wait_recv()
        f_high(s).start()

    def arrive_sides(s):
        f_low(s).wait_recv()
        f_high(s).wait_recv()

    def send_y(s):
        y_up(s).start()
        y_down(s).start()

    def send_s(s, which):
        for b in which:
            s_copy(s, b).start()

    def arrive_s(s):
        for b in range(boxes):
            s_copy(s, b).wait_recv()

    def wait_sends(s):
        for b in range(boxes):
            s_copy(s, b).wait_send()
        for copy in (y_up, y_down, f_low, f_high):
            copy(s).wait_send()

        @with_far
        def _():
            for b in range(boxes):
                x_copy(s, b).wait_send()
            c_up(s).wait_send()
            c_down(s).wait_send()

    codes = (3, 2 * 3 * (1 - core), 2 * 3 * core)

    def find_slots(b, carry):
        for line in (OWN, SIB, FAR):
            for place in range(3):
                slot = nearby
                for j in range(nearby):
                    slot = jnp.where(near[b, j] == codes[line] + place, j, slot)
                slots[b, 3 * line + place] = slot
        for blocks in (coupling, back):
            for part in range(2):
                blocks[b, part, nearby] = jnp.zeros(blocks.shape[3:], blocks.dtype)
        return carry


    def clear_far():
        def clear(i, carry):
            for h in range(2):
                for values in (skel, solved):
                    values[h * window + FAR * wide + i] = jnp.zeros(values.shape[1:], values.dtype)
            return carry

        lax.fori_loop(0, wide, clear, 0)

    lane = lax.broadcasted_iota(jnp.int32, (LANES, LANES), 1)

    def choose(ref, count, b):
        blocks = []
        names = ref[pl.ds(b, 1), :]
        for k in range(count // LANES):
            column = jnp.broadcast_to(names[:, k * LANES : (k + 1) * LANES], (LANES, LANES)).T
            pieces = [
                jnp.where(column == lane + m * LANES, 1.0, 0.0).astype(jnp.bfloat16) for m in range(M // LANES)
            ]
            blocks.append(jnp.concatenate(pieces, axis=1))
        return jnp.concatenate(blocks, axis=0)

    def halves(taken):
        for h in range(2):
            yield h, jnp.concatenate(
                [taken[:, h * half : (h + 1) * half], taken[:, (2 + h) * half : (3 + h) * half]], axis=1
            )

    def gather_skeleton(b):
        chosen = choose(skel_idx, K, b)
        load_fields(b).wait()
        taken = jnp.dot(chosen, fields[b], preferred_element_type=jnp.float32)
        for h, part in halves(taken):
            skel[h * window + OWN * wide + 1 + b] = part.astype(jnp.bfloat16)

    def gather_outer(i, carry):
        b = last * i
        gather_skeleton(b)

        @pl.when(i == 0)
        def _():
            pl.semaphore_wait(barrier, jnp.where(has_far, 4, 3))
            y_down(0).start()

        with_far(lambda: x_copy(0, b).start())
        pl.when(i == 1)(lambda: y_up(0).start())
        return carry

    def gather_inner(i, carry):
        gather_skeleton(1 + i)
        return carry

    def gather_redundant(b, carry):
        taken = jnp.dot(choose(red_idx, R, b), fields[b], preferred_element_type=jnp.float32)
        for h, part in halves(taken):
            partial[h * boxes + b, :R] = part
        return carry

    def make_placing(b, carry):
        names = jnp.concatenate([skel_idx[pl.ds(b, 1), :], red_idx[pl.ds(b, 1), :]], axis=1)
        rows = lax.broadcasted_iota(jnp.int32, (M, M), 0)
        placing[b] = jnp.where(rows == names, 1.0, 0.0).astype(jnp.bfloat16)
        return carry

    def matrix(blocks, b, places):
        found = [slots[b, place] for place in places]
        return jnp.concatenate(
            [jnp.concatenate([blocks[b, part, slot] for slot in found], axis=1) for part in range(2)], axis=0
        )

    def line_values(values, h, line, place, count):
        found = values[pl.ds(h * window + line * wide + place, count)]
        return found.reshape(count * found.shape[1], found.shape[2])

    def near_part(blocks, values, h, b):
        own = h * window + OWN * wide + b
        vectors = jnp.concatenate([values[own], values[own + 2], line_values(values, h, SIB, b, 3)], axis=0)
        places = (3 * OWN, 3 * OWN + 2, 3 * SIB, 3 * SIB + 1, 3 * SIB + 2)
        product = jnp.dot(matrix(blocks, b, places), vectors, preferred_element_type=jnp.float32)
        return to_complex(product, product.shape[0] // 2, half)

    def far_part(blocks, values, h, b, first=0, count=3):
        places = [3 * FAR + first + k for k in range(count)]
        vectors = line_values(values, h, FAR, b + first, count)
        product = jnp.dot(matrix(blocks, b, places), vectors, preferred_element_type=jnp.float32)
        return to_complex(product, product.shape[0] // 2, half)

    def solve_near(h, bs):
        for b in bs:
            partial[h * boxes + b, :R] -= near_part(coupling, skel, h, b)

    def solve_far(h, bs):
        targets = [
            (partial[h * boxes + b, :R] - far_part(coupling, skel, h, b)).astype(jnp.bfloat16) for b in bs
        ]
        for b, target in zip(bs, targets):
            full = jnp.dot(inverse[b].reshape(2 * R, R), target, preferred_element_type=jnp.float32)
            solved[h * window + OWN * wide + 1 + b] = to_complex(full, R, half).astype(jnp.bfloat16)

    def renew_near(h, bs):
        for b in bs:
            kept = skel[h * window + OWN * wide + 1 + b].astype(jnp.float32)
            partial[h * boxes + b] = kept - near_part(back, solved, h, b)

    def renew_sides(h):
        for b in outer:
            partial[h * boxes + b] -= far_part(back, solved, h, b, 1 if b == 0 else 0, 2)

    def renew_corners(h):
        place_renewed(h, outer, [partial[h * boxes + b] - far_part(back, solved, h, b, 0 if b == 0 else 2, 1) for b in outer])

    def renew_far(h, bs):
        place_renewed(h, bs, [partial[h * boxes + b] - far_part(back, solved, h, b) for b in bs])

    def place_renewed(h, bs, renewed):
        renewed = [kept.astype(jnp.bfloat16) for kept in renewed]
        for b, kept in zip(bs, renewed):
            stacked = jnp.concatenate([kept, solved[h * window + OWN * wide + 1 + b]], axis=0)
            placed = jnp.dot(placing[b], stacked, preferred_element_type=jnp.float32).astype(jnp.bfloat16)
            for part in range(2):
                result[b, :, (2 * part + h) * half : (2 * part + h + 1) * half] = placed[
                    :, part * half : (part + 1) * half
                ]

    loads[0].wait()
    lax.fori_loop(0, 2, gather_outer, 0)
    send_x(1, outer)
    send_y(1)
    for h in range(2):
        send_s(h, outer)
    lax.fori_loop(0, 2, gather_inner, 0)
    for h in range(2):
        send_s(h, inner)
    loads[1].wait()
    loads[2].wait()
    lax.fori_loop(0, boxes, gather_redundant, 0)
    pl.when(jnp.logical_not(has_far))(clear_far)
    lax.fori_loop(0, boxes, find_slots, 0)
    load_coupling.wait()
    arrive_s(0)
    solve_near(0, inner)
    corner_down(0)
    send_x(0, (1,))
    arrive_s(1)
    solve_near(1, inner)
    corner_up(0)
    send_x(0, (2,))
    lax.fori_loop(0, boxes, make_placing, 0)
    forward_sides(0)
    arrive_sides(0)
    corner_down(1)
    send_x(1, (1,))
    solve_near(0, outer)
    corner_up(1)
    send_x(1, (2,))
    forward_sides(1)
    arrive_sides(1)
    solve_near(1, outer)
    load_inverse.wait()
    arrive_x(0, inner)
    arrive_low_corner(0)
    arrive_high_corner(0)
    solve_far(0, outer)
    send_x(2, outer)
    send_y(2)
    send_s(2, outer)
    solve_far(0, inner)
    send_x(2, inner)
    send_s(2, inner)
    load_back.wait()
    arrive_s(2)
    renew_near(0, inner)
    arrive_x(1, inner)
    arrive_low_corner(1)
    arrive_high_corner(1)
    solve_far(1, outer)
    send_x(3, outer)
    send_y(3)
    send_s(3, outer)
    corner_down(2)
    solve_far(1, inner)
    send_x(3, inner)
    send_s(3, inner)
    corner_up(2)
    forward_sides(2)
    arrive_s(3)
    renew_near(1, inner)
    arrive_sides(2)
    renew_near(0, outer)
    arrive_x(2, inner)
    corner_down(3)
    renew_far(0, inner)
    corner_up(3)
    forward_sides(3)
    arrive_low_corner(2)
    arrive_high_corner(2)
    renew_far(0, outer)
    arrive_sides(3)
    renew_near(1, outer)
    arrive_x(3, inner)
    renew_far(1, inner)
    renew_sides(1)
    arrive_low_corner(3)
    arrive_high_corner(3)
    renew_corners(1)
    for s in range(4):
        wait_sends(s)


def on_device(
    rows_mesh, cols_mesh,
    fields, skeleton_index, redundant_index, neighbours, coupling, back_coupling, inverse,
):
    _, boxes, M, columns = fields.shape
    K, R, nearby = skeleton_index.shape[2], redundant_index.shape[2], neighbours.shape[2]
    bf16 = jnp.bfloat16
    wide = boxes + 2
    half = columns // 2
    far_memory = pl.BlockSpec(memory_space=pltpu.HBM)
    dma = pltpu.SemaphoreType.DMA
    out = pl.pallas_call(
        functools.partial(kernel, (rows_mesh, cols_mesh, boxes, K, R, nearby)),
        out_shape=pltpu.VMEM((boxes, M, columns), bf16),
        in_specs=[far_memory] * 7,
        out_specs=pl.BlockSpec(memory_space=pltpu.VMEM),
        scratch_shapes=[
            pltpu.VMEM((boxes, M, columns), bf16),
            pltpu.VMEM((boxes, K), jnp.int32),
            pltpu.VMEM((boxes, R), jnp.int32),
            pltpu.SMEM((boxes, nearby), jnp.int32),
            pltpu.VMEM((boxes, 2, nearby + 1, R, K), bf16),
            pltpu.VMEM((boxes, 2, nearby + 1, K, R), bf16),
            pltpu.VMEM((boxes, 2, R, R), bf16),
            pltpu.VMEM((2 * 3 * wide, K, half), bf16),
            pltpu.VMEM((2 * 3 * wide, R, half), bf16),
            pltpu.VMEM((boxes, M, M), bf16),
            pltpu.VMEM((2 * boxes, K, half), jnp.float32),
            pltpu.SMEM((boxes, 9), jnp.int32),
            dma((6,)), dma((boxes,)),
            dma((4, boxes)), dma((4, boxes)), dma((4, 2)), dma((4, 2)), dma((4, boxes)), dma((4, boxes)),
            dma((4, 2)), dma((4, 2)), dma((4, 2)), dma((4, 2)),
        ],
        compiler_params=pltpu.CompilerParams(
            collective_id=0, has_side_effects=True, vmem_limit_bytes=56 * 2**20
        ),
        cost_estimate=pl.CostEstimate(flops=14 * 10**9, bytes_accessed=25 * 10**6, transcendentals=0),
    )(
        fields.reshape(boxes, M, columns),
        skeleton_index.reshape(boxes, K),
        redundant_index.reshape(boxes, R),
        neighbours.reshape(boxes, nearby),
        coupling.reshape(boxes, 2, R, nearby, K).transpose(0, 1, 3, 2, 4),
        back_coupling.reshape(boxes, 2, K, nearby, R).transpose(0, 1, 3, 2, 4),
        inverse.reshape(boxes, 2, R, R),
    )
    return out.reshape(1, boxes, M, columns)


def solution(mesh):
    in_specs = (
        P("brow", "bcol", None, None),
        P("brow", "bcol", None),
        P("brow", "bcol", None),
        P("brow", "bcol", None),
        P("brow", "bcol", None, None, None, None),
        P("brow", "bcol", None, None, None, None),
        P("brow", "bcol", None, None, None),
    )
    out_specs = P("brow", "bcol", None, None)
    body = functools.partial(on_device, mesh.shape["brow"], mesh.shape["bcol"])
    return jax.shard_map(body, mesh=mesh, in_specs=in_specs, out_specs=out_specs, check_vma=False)
```

```python
import functools

import jax
import jax.numpy as jnp
from jax import lax
from jax.experimental import pallas as pl
from jax.experimental.pallas import tpu as pltpu
from jax.sharding import PartitionSpec as P

MESH = pl.DeviceIdType.MESH
LANES = 128
OWN, SIB, FAR = 0, 1, 2


def to_complex(product, rows, half):
    real_part = product[:rows, :half] - product[rows:, half:]
    imag_part = product[:rows, half:] + product[rows:, :half]
    return jnp.concatenate([real_part, imag_part], axis=1)


def kernel(
    sizes,
    fields_hbm, skel_hbm, red_hbm, near_hbm, coupling_hbm, back_hbm, inverse_hbm,
    result,
    fields, skel_idx, red_idx, near, coupling, back, inverse, skel, solved, placing, partial, slots,
    load_sem, field_sem,
    x_send, x_recv, y_send, y_recv, s_send, s_recv, c_send, c_recv, f_send, f_recv,
):
    rows_mesh, cols_mesh, boxes, K, R, nearby = sizes
    M = K + R
    wide = boxes + 2
    window = 3 * wide
    last = boxes - 1
    half = LANES

    row, col = lax.axis_index("brow"), lax.axis_index("bcol")
    core = lax.rem(row, 2)
    sibling = row + 1 - 2 * core
    across = row - 1 + 2 * core
    has_far = jnp.logical_and(across >= 0, across < rows_mesh)
    up, down = lax.rem(col + 1, cols_mesh), lax.rem(col + cols_mesh - 1, cols_mesh)
    at_sibling, at_far, at_up, at_down = (sibling, col), (across, col), (row, up), (row, down)

    barrier = pltpu.get_barrier_semaphore()
    for device in (at_sibling, at_up, at_down):
        pl.semaphore_signal(barrier, inc=1, device_id=device, device_id_type=MESH)

    @pl.when(has_far)
    def _():
        pl.semaphore_signal(barrier, inc=1, device_id=at_far, device_id_type=MESH)

    def load_fields(b):
        return pltpu.make_async_copy(fields_hbm.at[b], fields.at[b], field_sem.at[b])

    loads = [
        pltpu.make_async_copy(source, target, load_sem.at[3 + k])
        for k, (source, target) in enumerate(((skel_hbm, skel_idx), (red_hbm, red_idx), (near_hbm, near)))
    ]
    for load in loads:
        load.start()
    inner, outer = (1, 2), (0, last)
    for b in (*outer, *inner):
        load_fields(b).start()
    named = pl.ds(0, nearby)
    load_inverse = pltpu.make_async_copy(inverse_hbm, inverse, load_sem.at[0])
    load_coupling = pltpu.make_async_copy(coupling_hbm, coupling.at[:, :, named], load_sem.at[1])
    load_back = pltpu.make_async_copy(back_hbm, back.at[:, :, named], load_sem.at[2])
    load_coupling.start()
    load_inverse.start()
    load_back.start()

    def remote(stage, source, target, device, send, recv):
        values, base = (skel, solved)[stage // 2], (stage % 2) * window
        return pltpu.make_async_remote_copy(
            src_ref=values.at[base + source], dst_ref=values.at[base + target], send_sem=send, recv_sem=recv,
            device_id=device, device_id_type=MESH,
        )

    def x_copy(s, b):
        return remote(s, OWN * wide + 1 + b, FAR * wide + 1 + b, at_far, x_send.at[s, b], x_recv.at[s, b])

    def y_up(s):
        return remote(s, OWN * wide + boxes, OWN * wide, at_up, y_send.at[s, 0], y_recv.at[s, 0])

    def y_down(s):
        return remote(s, OWN * wide + 1, OWN * wide + boxes + 1, at_down, y_send.at[s, 1], y_recv.at[s, 1])

    def s_copy(s, b):
        return remote(s, OWN * wide + 1 + b, SIB * wide + 1 + b, at_sibling, s_send.at[s, b], s_recv.at[s, b])

    def c_up(s):
        return remote(s, FAR * wide + boxes, FAR * wide, at_up, c_send.at[s, 0], c_recv.at[s, 0])

    def c_down(s):
        return remote(s, FAR * wide + 1, FAR * wide + boxes + 1, at_down, c_send.at[s, 1], c_recv.at[s, 1])

    def f_low(s):
        return remote(s, OWN * wide, SIB * wide, at_sibling, f_send.at[s, 0], f_recv.at[s, 0])

    def f_high(s):
        return remote(s, OWN * wide + last + 2, SIB * wide + last + 2, at_sibling, f_send.at[s, 1], f_recv.at[s, 1])

    def with_far(action):
        pl.when(has_far)(action)

    def send_x(s, which):
        @with_far
        def _():
            for b in which:
                x_copy(s, b).start()

    def arrive_x(s, which):
        @with_far
        def _():
            for b in which:
                x_copy(s, b).wait_recv()

    def corner_down(s):
        @with_far
        def _():
            x_copy(s, 0).wait_recv()
            c_down(s).start()

    def corner_up(s):
        @with_far
        def _():
            x_copy(s, last).wait_recv()
            c_up(s).start()

    def arrive_low_corner(s):
        with_far(lambda: c_up(s).wait_recv())

    def arrive_high_corner(s):
        with_far(lambda: c_down(s).wait_recv())

    def forward_sides(s):
        y_up(s).wait_recv()
        f_low(s).start()
        y_down(s).wait_recv()
        f_high(s).start()

    def arrive_sides(s):
        f_low(s).wait_recv()
        f_high(s).wait_recv()

    def send_y(s):
        y_up(s).start()
        y_down(s).start()

    def send_s(s, which):
        for b in which:
            s_copy(s, b).start()

    def arrive_s(s):
        for b in range(boxes):
            s_copy(s, b).wait_recv()

    def wait_sends(s):
        for b in range(boxes):
            s_copy(s, b).wait_send()
        for copy in (y_up, y_down, f_low, f_high):
            copy(s).wait_send()

        @with_far
        def _():
            for b in range(boxes):
                x_copy(s, b).wait_send()
            c_up(s).wait_send()
            c_down(s).wait_send()

    codes = (3, 2 * 3 * (1 - core), 2 * 3 * core)

    def find_slots(b, carry):
        for line in (OWN, SIB, FAR):
            for place in range(3):
                slot = nearby
                for j in range(nearby):
                    slot = jnp.where(near[b, j] == codes[line] + place, j, slot)
                slots[b, 3 * line + place] = slot
        for blocks in (coupling, back):
            for part in range(2):
                blocks[b, part, nearby] = jnp.zeros(blocks.shape[3:], blocks.dtype)
        return carry


    def clear_far():
        def clear(i, carry):
            for h in range(2):
                for values in (skel, solved):
                    values[h * window + FAR * wide + i] = jnp.zeros(values.shape[1:], values.dtype)
            return carry

        lax.fori_loop(0, wide, clear, 0)

    lane = lax.broadcasted_iota(jnp.int32, (LANES, LANES), 1)

    def choose(ref, count, b):
        blocks = []
        names = ref[pl.ds(b, 1), :]
        for k in range(count // LANES):
            column = jnp.broadcast_to(names[:, k * LANES : (k + 1) * LANES], (LANES, LANES)).T
            pieces = [
                jnp.where(column == lane + m * LANES, 1.0, 0.0).astype(jnp.bfloat16) for m in range(M // LANES)
            ]
            blocks.append(jnp.concatenate(pieces, axis=1))
        return jnp.concatenate(blocks, axis=0)

    def halves(taken):
        for h in range(2):
            yield h, jnp.concatenate(
                [taken[:, h * half : (h + 1) * half], taken[:, (2 + h) * half : (3 + h) * half]], axis=1
            )

    def gather_skeleton(b):
        chosen = choose(skel_idx, K, b)
        load_fields(b).wait()
        taken = jnp.dot(chosen, fields[b], preferred_element_type=jnp.float32)
        for h, part in halves(taken):
            skel[h * window + OWN * wide + 1 + b] = part.astype(jnp.bfloat16)

    def gather_outer(i, carry):
        b = last * i
        gather_skeleton(b)

        @pl.when(i == 0)
        def _():
            pl.semaphore_wait(barrier, jnp.where(has_far, 4, 3))
            y_down(0).start()

        with_far(lambda: x_copy(0, b).start())
        pl.when(i == 1)(lambda: y_up(0).start())
        return carry

    def gather_inner(i, carry):
        gather_skeleton(1 + i)
        return carry

    def gather_redundant(b, carry):
        taken = jnp.dot(choose(red_idx, R, b), fields[b], preferred_element_type=jnp.float32)
        for h, part in halves(taken):
            partial[h * boxes + b, :R] = part
        return carry

    def make_placing(b, carry):
        names = jnp.concatenate([skel_idx[pl.ds(b, 1), :], red_idx[pl.ds(b, 1), :]], axis=1)
        rows = lax.broadcasted_iota(jnp.int32, (M, M), 0)
        placing[b] = jnp.where(rows == names, 1.0, 0.0).astype(jnp.bfloat16)
        return carry

    def matrix(blocks, b, places):
        found = [slots[b, place] for place in places]
        return jnp.concatenate(
            [jnp.concatenate([blocks[b, part, slot] for slot in found], axis=1) for part in range(2)], axis=0
        )

    def line_values(values, h, line, place, count):
        found = values[pl.ds(h * window + line * wide + place, count)]
        return found.reshape(count * found.shape[1], found.shape[2])

    def near_part(blocks, values, h, b):
        own = h * window + OWN * wide + b
        vectors = jnp.concatenate([values[own], values[own + 2], line_values(values, h, SIB, b, 3)], axis=0)
        places = (3 * OWN, 3 * OWN + 2, 3 * SIB, 3 * SIB + 1, 3 * SIB + 2)
        product = jnp.dot(matrix(blocks, b, places), vectors, preferred_element_type=jnp.float32)
        return to_complex(product, product.shape[0] // 2, half)

    def far_part(blocks, values, h, b, first=0, count=3):
        places = [3 * FAR + first + k for k in range(count)]
        vectors = line_values(values, h, FAR, b + first, count)
        product = jnp.dot(matrix(blocks, b, places), vectors, preferred_element_type=jnp.float32)
        return to_complex(product, product.shape[0] // 2, half)

    def solve_near(h, bs):
        for b in bs:
            partial[h * boxes + b, :R] -= near_part(coupling, skel, h, b)

    def solve_far(h, bs):
        targets = [
            (partial[h * boxes + b, :R] - far_part(coupling, skel, h, b)).astype(jnp.bfloat16) for b in bs
        ]
        for b, target in zip(bs, targets):
            full = jnp.dot(inverse[b].reshape(2 * R, R), target, preferred_element_type=jnp.float32)
            solved[h * window + OWN * wide + 1 + b] = to_complex(full, R, half).astype(jnp.bfloat16)

    def renew_near(h, bs):
        for b in bs:
            kept = skel[h * window + OWN * wide + 1 + b].astype(jnp.float32)
            partial[h * boxes + b] = kept - near_part(back, solved, h, b)

    def renew_sides(h):
        for b in outer:
            partial[h * boxes + b] -= far_part(back, solved, h, b, 1 if b == 0 else 0, 2)

    def renew_corners(h):
        place_renewed(h, outer, [partial[h * boxes + b] - far_part(back, solved, h, b, 0 if b == 0 else 2, 1) for b in outer])

    def renew_far(h, bs):
        place_renewed(h, bs, [partial[h * boxes + b] - far_part(back, solved, h, b) for b in bs])

    def place_renewed(h, bs, renewed):
        renewed = [kept.astype(jnp.bfloat16) for kept in renewed]
        for b, kept in zip(bs, renewed):
            stacked = jnp.concatenate([kept, solved[h * window + OWN * wide + 1 + b]], axis=0)
            placed = jnp.dot(placing[b], stacked, preferred_element_type=jnp.float32).astype(jnp.bfloat16)
            for part in range(2):
                result[b, :, (2 * part + h) * half : (2 * part + h + 1) * half] = placed[
                    :, part * half : (part + 1) * half
                ]

    loads[0].wait()
    lax.fori_loop(0, 2, gather_outer, 0)
    send_x(1, outer)
    send_y(1)
    for h in range(2):
        send_s(h, outer)
    lax.fori_loop(0, 2, gather_inner, 0)
    for h in range(2):
        send_s(h, inner)
    loads[1].wait()
    loads[2].wait()
    lax.fori_loop(0, boxes, gather_redundant, 0)
    pl.when(jnp.logical_not(has_far))(clear_far)
    lax.fori_loop(0, boxes, find_slots, 0)
    load_coupling.wait()
    arrive_s(0)
    solve_near(0, inner)
    corner_down(0)
    send_x(0, (1,))
    arrive_s(1)
    solve_near(1, inner)
    corner_up(0)
    send_x(0, (2,))
    lax.fori_loop(0, boxes, make_placing, 0)
    forward_sides(0)
    arrive_sides(0)
    corner_down(1)
    send_x(1, (1,))
    solve_near(0, outer)
    corner_up(1)
    send_x(1, (2,))
    forward_sides(1)
    arrive_sides(1)
    solve_near(1, outer)
    load_inverse.wait()
    arrive_x(0, inner)
    arrive_low_corner(0)
    arrive_high_corner(0)
    solve_far(0, outer)
    send_x(2, outer)
    send_y(2)
    send_s(2, outer)
    solve_far(0, inner)
    send_x(2, inner)
    send_s(2, inner)
    load_back.wait()
    arrive_s(2)
    renew_near(0, inner)
    arrive_x(1, inner)
    arrive_low_corner(1)
    arrive_high_corner(1)
    solve_far(1, outer)
    send_x(3, outer)
    send_y(3)
    send_s(3, outer)
    corner_down(2)
    solve_far(1, inner)
    send_x(3, inner)
    send_s(3, inner)
    corner_up(2)
    forward_sides(2)
    arrive_s(3)
    renew_near(1, inner)
    arrive_sides(2)
    renew_near(0, outer)
    arrive_x(2, inner)
    corner_down(3)
    corner_up(3)
    renew_far(0, inner)
    forward_sides(3)
    arrive_low_corner(2)
    arrive_high_corner(2)
    renew_far(0, outer)
    arrive_sides(3)
    renew_near(1, outer)
    arrive_x(3, inner)
    renew_far(1, inner)
    renew_sides(1)
    arrive_low_corner(3)
    arrive_high_corner(3)
    renew_corners(1)
    for s in range(4):
        wait_sends(s)


def on_device(
    rows_mesh, cols_mesh,
    fields, skeleton_index, redundant_index, neighbours, coupling, back_coupling, inverse,
):
    _, boxes, M, columns = fields.shape
    K, R, nearby = skeleton_index.shape[2], redundant_index.shape[2], neighbours.shape[2]
    bf16 = jnp.bfloat16
    wide = boxes + 2
    half = columns // 2
    far_memory = pl.BlockSpec(memory_space=pltpu.HBM)
    dma = pltpu.SemaphoreType.DMA
    out = pl.pallas_call(
        functools.partial(kernel, (rows_mesh, cols_mesh, boxes, K, R, nearby)),
        out_shape=pltpu.VMEM((boxes, M, columns), bf16),
        in_specs=[far_memory] * 7,
        out_specs=pl.BlockSpec(memory_space=pltpu.VMEM),
        scratch_shapes=[
            pltpu.VMEM((boxes, M, columns), bf16),
            pltpu.VMEM((boxes, K), jnp.int32),
            pltpu.VMEM((boxes, R), jnp.int32),
            pltpu.SMEM((boxes, nearby), jnp.int32),
            pltpu.VMEM((boxes, 2, nearby + 1, R, K), bf16),
            pltpu.VMEM((boxes, 2, nearby + 1, K, R), bf16),
            pltpu.VMEM((boxes, 2, R, R), bf16),
            pltpu.VMEM((2 * 3 * wide, K, half), bf16),
            pltpu.VMEM((2 * 3 * wide, R, half), bf16),
            pltpu.VMEM((boxes, M, M), bf16),
            pltpu.VMEM((2 * boxes, K, half), jnp.float32),
            pltpu.SMEM((boxes, 9), jnp.int32),
            dma((6,)), dma((boxes,)),
            dma((4, boxes)), dma((4, boxes)), dma((4, 2)), dma((4, 2)), dma((4, boxes)), dma((4, boxes)),
            dma((4, 2)), dma((4, 2)), dma((4, 2)), dma((4, 2)),
        ],
        compiler_params=pltpu.CompilerParams(
            collective_id=0, has_side_effects=True, vmem_limit_bytes=56 * 2**20
        ),
        cost_estimate=pl.CostEstimate(flops=14 * 10**9, bytes_accessed=25 * 10**6, transcendentals=0),
    )(
        fields.reshape(boxes, M, columns),
        skeleton_index.reshape(boxes, K),
        redundant_index.reshape(boxes, R),
        neighbours.reshape(boxes, nearby),
        coupling.reshape(boxes, 2, R, nearby, K).transpose(0, 1, 3, 2, 4),
        back_coupling.reshape(boxes, 2, K, nearby, R).transpose(0, 1, 3, 2, 4),
        inverse.reshape(boxes, 2, R, R),
    )
    return out.reshape(1, boxes, M, columns)


def solution(mesh):
    in_specs = (
        P("brow", "bcol", None, None),
        P("brow", "bcol", None),
        P("brow", "bcol", None),
        P("brow", "bcol", None),
        P("brow", "bcol", None, None, None, None),
        P("brow", "bcol", None, None, None, None),
        P("brow", "bcol", None, None, None),
    )
    out_specs = P("brow", "bcol", None, None)
    body = functools.partial(on_device, mesh.shape["brow"], mesh.shape["bcol"])
    return jax.shard_map(body, mesh=mesh, in_specs=in_specs, out_specs=out_specs, check_vma=False)
```
